128 devices in a mesh: rep: 8 (over z, core), fsdp: 16 (over x, y).
Axes of the slice: x: 4, y: 4, z: 4, core: 2. Of those that a mesh axis runs over, the one named last changes fastest.
Arguments:
- grad: bfloat16 [8, 2, 8192, 1024], P('rep', None, 'fsdp'), may hold values from -6 to 6
- error: float32 [8, 2, 8192, 1024], P('rep', None, 'fsdp'), may hold values from -6 to 6
- momentum: float32 [8, 2, 8192, 1024], P('rep', None, 'fsdp'), may hold values from -90 to 90
- warm_start: float32 [2, 1024, 64], replicated, may hold values from -6 to 6
Outputs:
- error_next: float32 [8, 2, 8192, 1024], P('rep', None, 'fsdp')
- momentum_next: float32 [8, 2, 8192, 1024], P('rep', None, 'fsdp')
- update: float32 [2, 8192, 1024], P(None, 'fsdp')
- basis_next: float32 [2, 1024, 64], replicated
The draws below stay inside these ranges and needn't reach their ends.
All inputs are finite; a program needn't handle non-finite values.
Results may differ from the reference program's by a relative error of at most 0.0003.
Values sent between devices are 32-bit elements; how exact they have to be, the bound alone decides.
A program may use at most 128 MiB of HBM per device.

```python
import math
import jax
import jax.numpy as jnp
from jax import lax

D = 8192
KVW = 1024
R = 64
PROJ = 2
ITERS = 2
REPLICAS = 8
N_REP = 8


def draw_momentum(key, part):
    key = jax.random.fold_in(key, 7)
    keys = jax.random.split(key, 3)
    shape = (N_REP, PROJ, D, KVW)
    rising = 3.0 ** (jnp.arange(D, dtype=jnp.float32) / D)
    row_scale = rising[None, :, None] * jnp.exp(jax.random.uniform(keys[1], (PROJ, D, 1)) * math.log(10.0))
    col_scale = jnp.exp(jax.random.uniform(keys[2], (PROJ, 1, KVW)) * math.log(10.0))
    base = jnp.clip(jax.random.normal(keys[0], shape), -6.0, 6.0)
    return (0.05 * base * row_scale[None] * col_scale[None]).astype(jnp.float32)


def shard_levels(stream_key, shape, pieces, least, top_value):
    level, own = 1.0, jax.random.fold_in(stream_key, 6)
    for dim, shards_of in pieces:
        steps = jnp.exp(jax.random.uniform(jax.random.fold_in(own, dim), (shards_of,), jnp.float32, least / len(pieces), top_value / len(pieces)))
        level = level * jnp.repeat(steps, shape[dim] // shards_of).reshape([-1 if axis == dim else 1 for axis in range(len(shape))])
    return level


def scatter_about(key, extent, scale, limit, cuts=(), held_as=jnp.bfloat16):
    result = scale * jax.random.normal(key, extent, jnp.float32)
    if cuts:
        result = result * shard_levels(key, extent, cuts, -0.22, 0.18)
    return jnp.clip(result, -limit, limit).astype(held_as)


def setup_inputs(seed: int = 0) -> dict:
    arg_keys = jax.random.split(jax.random.key(seed), 5)
    grad = scatter_about(arg_keys[0], (REPLICAS, PROJ, D, KVW), 1.0, 6.0, ((0, 8), (2, 16)))
    error = scatter_about(arg_keys[1], (REPLICAS, PROJ, D, KVW), 0.5, 6.0, ((0, 8), (2, 16)), jnp.float32)
    momentum = draw_momentum(jax.random.fold_in(arg_keys[4], 71), 0)
    warm_start = scatter_about(arg_keys[3], (PROJ, KVW, R), 1.0, 6.0, (), jnp.float32)
    return dict(grad=grad, error=error, momentum=momentum, warm_start=warm_start)


def orthonormalise(factor, gram_matrix):
    width = gram_matrix.shape[-1]
    trace_value = jnp.trace(gram_matrix, axis1=1, axis2=2)
    ridge_term = (0.0001 * trace_value / width)[:, None, None] * jnp.eye(width, dtype=jnp.float32)
    lower_factor = jnp.linalg.cholesky(gram_matrix + ridge_term)
    return lax.linalg.triangular_solve(lower_factor, factor, left_side=False, lower=True, transpose_a=True)

def reference(grad, error, momentum, warm_start):
    momentum_next = 0.9 * momentum + grad.astype(jnp.float32)
    merged = momentum_next + error
    basis = warm_start
    unit_rows = None
    for iteration in range(ITERS):
        factor = jnp.einsum('rpdc,pck->pdk', merged, basis, precision=lax.Precision.HIGHEST) / N_REP
        gram_matrix = jnp.einsum('pdk,pdl->pkl', factor, factor, precision=lax.Precision.HIGHEST)
        unit_rows = orthonormalise(factor, gram_matrix)
        basis = jnp.einsum('rpdc,pdk->pck', merged, unit_rows, precision=lax.Precision.HIGHEST) / N_REP
    update = jnp.einsum('pdk,pck->pdc', unit_rows, basis, precision=lax.Precision.HIGHEST)
    error_next = merged - update[None]
    return (error_next, momentum_next, update, basis)
```

```python
import functools

import jax
import jax.numpy as jnp
from jax import lax
from jax.experimental import pallas as pl
from jax.experimental.pallas import tpu as pltpu
from jax.sharding import PartitionSpec as P

MESH = pl.DeviceIdType.MESH
f32 = jnp.float32
bf16 = jnp.bfloat16

RANK = 64
ROWS = 512
COLS = 1024
CHUNK = 128
CHUNKS = ROWS // CHUNK
CHIPS = 64
SELF = 42
NN = (((1,), (0,)), ((), ()))
NT = (((1,), (1,)), ((), ()))
TN = (((0,), (0,)), ((), ()))


def split3(x):
    high = x.astype(bf16)
    rest = x - high.astype(f32)
    mid = rest.astype(bf16)
    low = (rest - mid.astype(f32)).astype(bf16)
    return high, mid, low


def dot6(a, w, dims):
    n = a[0].shape[0]
    dot = functools.partial(lax.dot_general, dimension_numbers=dims, preferred_element_type=f32)
    s1 = dot(jnp.concatenate(a, axis=0), w[0])
    s2 = dot(jnp.concatenate(a[:2], axis=0), w[1])
    s3 = dot(a[0], w[2])
    return ((s1[2 * n:] + s2[n:]) + s3) + (s1[n:2 * n] + s2[:n]) + s1[:n]


def inverse_lower_factor(gram):
    n = RANK
    row_id = lax.broadcasted_iota(jnp.int32, (n, n), 0)
    col_id = lax.broadcasted_iota(jnp.int32, (n, n), 1)
    diagonal = row_id == col_id
    trace = jnp.sum(jnp.where(diagonal, gram, 0.0))
    a = jnp.concatenate(
        [gram + jnp.where(diagonal, 0.0001 * trace / n, 0.0), jnp.where(diagonal, 1.0, 0.0).astype(f32)], axis=1)
    rows = []
    for k in range(n):
        low = (k // 8) * 8
        a = a[low - (n - a.shape[0]):]
        at = k - low
        inv = lax.rsqrt(a[at:at + 1, k:k + 1])
        row = a[at:at + 1, :] * inv
        rows.append(row)
        col = a[:, k:k + 1] * inv
        below = lax.broadcasted_iota(jnp.int32, a.shape, 0) > at
        a = a - jnp.where(below, col * row, 0.0)
    return jnp.concatenate(rows, axis=0)[:, n:]


def iterate_kernel(grad, error, momentum, warm, unit_out, basis_out,
                   g_buf, e_buf, m_buf, away, home, landed, parts, warm_parts,
                   f_slots, y_tiles, y_terms, y_full, g_slots, mine_out, theirs_unit, theirs_basis,
                   load_sem, swap_send, swap_recv, f_send, f_recv, rs_send, rs_recv, ag_send, ag_recv,
                   gram_send, gram_recv, end_send, end_recv):
    rep = lax.axis_index("rep")
    fsdp = lax.axis_index("fsdp")
    z, core = rep // 2, lax.rem(rep, 2)
    x, y = fsdp // 4, lax.rem(fsdp, 4)
    chip = z * 16 + fsdp
    partner = (rep + 1 - 2 * core, fsdp)

    def load(role, q):
        p = core if role else 1 - core
        rows = pl.ds(q * CHUNK, CHUNK)
        return [
            pltpu.make_async_copy(ref.at[0, p, rows], buf.at[role, rows], load_sem.at[i, role, q])
            for i, (ref, buf) in enumerate(((grad, g_buf), (error, e_buf), (momentum, m_buf)))
        ]

    for q in range(CHUNKS):
        for role in range(2):
            for copy in load(role, q):
                copy.start()

    def peer(k):
        pz = lax.rem(z + 2 + k // 16, 4)
        px = lax.rem(x + 2 + lax.rem(k // 4, 4), 4)
        py = lax.rem(y + 2 + lax.rem(k, 4), 4)
        return pz, px * 4 + py

    def each_peer(body):
        def step(k, carry):
            body(k)
            return carry
        lax.fori_loop(0, SELF, step, 0)
        lax.fori_loop(SELF + 1, CHIPS, step, 0)

    barrier = pltpu.get_barrier_semaphore()

    def greet(k):
        pz, pf = peer(k)
        pl.semaphore_signal(barrier, inc=1, device_id=(pz * 2 + core, pf), device_id_type=MESH)

    each_peer(greet)
    pl.semaphore_signal(barrier, inc=1, device_id=partner, device_id_type=MESH)

    for i, part in enumerate(zip(split3(warm[0]), split3(warm[1]))):
        warm_parts[i] = jnp.where(core == 0, part[0].astype(f32), part[1].astype(f32)).astype(bf16)

    pl.semaphore_wait(barrier, CHIPS)

    def swap(q):
        rows = pl.ds(q * CHUNK, CHUNK)
        return pltpu.make_async_remote_copy(
            src_ref=away.at[rows], dst_ref=landed.at[rows], send_sem=swap_send.at[q], recv_sem=swap_recv.at[q],
            device_id=partner, device_id_type=MESH)

    def merged(role, q):
        for copy in load(role, q):
            copy.wait()
        rows = slice(q * CHUNK, (q + 1) * CHUNK)
        return (0.9 * m_buf[role, rows] + g_buf[role, rows].astype(f32)) + e_buf[role, rows]

    def f_copy(it, q, dz):
        block = f_slots.at[it, z, :, pl.ds(q * CHUNK, CHUNK)]
        pz = lax.rem(z + dz, 4)
        return pltpu.make_async_remote_copy(
            src_ref=block, dst_ref=block, send_sem=f_send.at[it, q, dz - 1], recv_sem=f_recv.at[it, q],
            device_id=(pz * 2 + core, fsdp), device_id_type=MESH)

    def f_all(it, q):
        three = f_slots.at[it, pl.ds(0, 3), :, pl.ds(q * CHUNK, CHUNK)]
        return pltpu.make_async_copy(three, three, f_recv.at[it, q])

    def send_factor(it, q, value):
        f_slots[it, z, :, q * CHUNK:(q + 1) * CHUNK] = value
        for dz in (2, 1, 3):
            f_copy(it, q, dz).start()

    for q in range(CHUNKS):
        away[q * CHUNK:(q + 1) * CHUNK] = merged(0, q)
        swap(q).start()
        home[q * CHUNK:(q + 1) * CHUNK] = merged(1, q)

    for q in range(CHUNKS):
        rows = slice(q * CHUNK, (q + 1) * CHUNK)
        swap(q).wait_recv()
        block = split3((home[rows] + landed[rows]) * 0.125)
        for i in range(3):
            parts[i, rows] = block[i]
        send_factor(0, q, dot6([warm_parts[i] for i in range(3)], block, NT))

    def gram_copy(it, k):
        px = lax.rem(x + 2 + k // 4, 4)
        py = lax.rem(y + 2 + lax.rem(k, 4), 4)
        return pltpu.make_async_remote_copy(
            src_ref=g_slots.at[it, fsdp], dst_ref=g_slots.at[it, fsdp],
            send_sem=gram_send.at[it], recv_sem=gram_recv.at[it],
            device_id=(rep, px * 4 + py), device_id_type=MESH)

    def each_plane(body):
        def step(k, carry):
            body(k)
            return carry
        lax.fori_loop(0, 10, step, 0)
        lax.fori_loop(11, 16, step, 0)

    def rs_copy(it, k):
        pz, pf = peer(k)
        return pltpu.make_async_remote_copy(
            src_ref=y_tiles.at[it, pz * 16 + pf], dst_ref=y_terms.at[it, k],
            send_sem=rs_send.at[it], recv_sem=rs_recv.at[it], device_id=(pz * 2 + core, pf), device_id_type=MESH)

    def ag_copy(it, k):
        pz, pf = peer(k)
        return pltpu.make_async_remote_copy(
            src_ref=y_full.at[it, chip], dst_ref=y_full.at[it, chip],
            send_sem=ag_send.at[it], recv_sem=ag_recv.at[it], device_id=(pz * 2 + core, pf), device_id_type=MESH)

    def all_of(ref, sem):
        return pltpu.make_async_copy(ref, ref, sem)

    all_parts = lambda: [parts[i] for i in range(3)]
    for it in range(2):
        for q in range(CHUNKS):
            f_all(it, q).wait()
        factor = jnp.sum(f_slots[it], axis=0)
        factor_parts = split3(factor)
        gram = dot6(factor_parts, factor_parts, NT)
        g_slots[it, fsdp] = jnp.concatenate([gram[:32], gram[32:]], axis=1)
        each_plane(lambda k: gram_copy(it, k).start())

        term = dot6(factor_parts, all_parts(), NN)
        for a in range(8):
            for b in range(8):
                y_tiles[it, a * 8 + b] = term[a * 8:(a + 1) * 8, b * 128:(b + 1) * 128]
        y_terms[it, SELF] = y_tiles[it, chip]
        each_peer(lambda k: rs_copy(it, k).start())
        all_of(y_terms.at[it, pl.ds(0, CHIPS - 1)], rs_recv.at[it]).wait()
        y_full[it, chip] = jnp.sum(y_terms[it], axis=0)
        each_peer(lambda k: ag_copy(it, k).start())

        all_of(g_slots.at[it, pl.ds(0, 15)], gram_recv.at[it]).wait()
        packed = jnp.sum(g_slots[it], axis=0)
        inverse = inverse_lower_factor(jnp.concatenate([packed[:, :RANK], packed[:, RANK:]], axis=0))
        inverse_parts = split3(inverse)
        if it == 1:
            unit = dot6(inverse_parts, factor_parts, NN)
            unit_out[core] = unit
            mine_out[:, COLS:] = unit
            unit_copy = pltpu.make_async_remote_copy(
                src_ref=mine_out.at[:, pl.ds(COLS, ROWS)], dst_ref=theirs_unit,
                send_sem=end_send.at[0], recv_sem=end_recv.at[0], device_id=partner, device_id_type=MESH)
            unit_copy.start()

        all_of(y_full.at[it, pl.ds(0, CHIPS - 1)], ag_recv.at[it]).wait()
        total = jnp.concatenate(
            [jnp.concatenate([y_full[it, a * 8 + b] for b in range(8)], axis=1) for a in range(8)], axis=0)
        basis = dot6(inverse_parts, split3(total), NN)
        if it == 0:
            basis_parts = split3(basis)
            for q in range(CHUNKS):
                rows = slice(q * CHUNK, (q + 1) * CHUNK)
                send_factor(1, q, dot6(basis_parts, [parts[i, rows] for i in range(3)], NT))

    mine_out[:, :COLS] = basis
    basis_copy = pltpu.make_async_remote_copy(
        src_ref=mine_out.at[:, pl.ds(0, COLS)], dst_ref=theirs_basis,
        send_sem=end_send.at[1], recv_sem=end_recv.at[1], device_id=partner, device_id_type=MESH)
    basis_copy.start()
    basis_out[core] = basis
    unit_copy.wait_recv()
    unit_out[1 - core] = theirs_unit[...]

    for q in range(CHUNKS):
        swap(q).wait_send()
    for it in range(2):
        for q in range(CHUNKS):
            for dz in (1, 2, 3):
                f_copy(it, q, dz).wait_send()
        all_of(y_terms.at[it, pl.ds(0, CHIPS - 1)], rs_send.at[it]).wait()
        all_of(y_full.at[it, pl.ds(0, CHIPS - 1)], ag_send.at[it]).wait()
        all_of(g_slots.at[it, pl.ds(0, 15)], gram_send.at[it]).wait()
    unit_copy.wait_send()
    basis_copy.wait()
    basis_out[1 - core] = theirs_basis[...]


def iterate(grad, error, momentum, warm):
    vmem = pl.BlockSpec(memory_space=pltpu.VMEM)
    hbm = pl.BlockSpec(memory_space=pl.ANY)
    dma = pltpu.SemaphoreType.DMA
    return pl.pallas_call(
        iterate_kernel,
        out_shape=(jax.ShapeDtypeStruct((2, RANK, ROWS), f32), jax.ShapeDtypeStruct((2, RANK, COLS), f32)),
        in_specs=[hbm, hbm, hbm, vmem],
        out_specs=(vmem, vmem),
        scratch_shapes=[
            pltpu.VMEM((2, ROWS, COLS), bf16),
            pltpu.VMEM((2, ROWS, COLS), f32),
            pltpu.VMEM((2, ROWS, COLS), f32),
            pltpu.VMEM((ROWS, COLS), f32),
            pltpu.VMEM((ROWS, COLS), f32),
            pltpu.VMEM((ROWS, COLS), f32),
            pltpu.VMEM((3, ROWS, COLS), bf16),
            pltpu.VMEM((3, RANK, COLS), bf16),
            pltpu.VMEM((2, 4, RANK, ROWS), f32),
            pltpu.VMEM((2, CHIPS, 8, 128), f32),
            pltpu.VMEM((2, CHIPS, 8, 128), f32),
            pltpu.VMEM((2, CHIPS, 8, 128), f32),
            pltpu.VMEM((2, 16, 32, 128), f32),
            pltpu.VMEM((RANK, COLS + ROWS), f32),
            pltpu.VMEM((RANK, ROWS), f32),
            pltpu.VMEM((RANK, COLS), f32),
            dma((3, 2, CHUNKS)),
            dma((CHUNKS,)), dma((CHUNKS,)),
            dma((2, CHUNKS, 3)), dma((2, CHUNKS)),
            dma((2,)), dma((2,)),
            dma((2,)), dma((2,)),
            dma((2,)), dma((2,)),
            dma((2,)), dma((2,)),
        ],
        compiler_params=pltpu.CompilerParams(
            collective_id=0, has_side_effects=True, vmem_limit_bytes=40 * 2**20),
        name="power_iterations",
    )(grad, error, momentum, warm)


def finish_kernel(grad, error, momentum, unit, basis, error_next, momentum_next, update, basis_next):
    @pl.when((pl.program_id(0) == 0) & (pl.program_id(1) == 0))
    def _():
        basis_next[...] = basis[...]

    p = pl.program_id(0)
    u = split3(unit[0])
    b = split3(basis[p])
    left = jnp.concatenate([u[0], u[0], u[1], u[0], u[2], u[1]], axis=0)
    right = jnp.concatenate([b[0], b[1], b[0], b[2], b[0], b[1]], axis=0)
    delta = lax.dot_general(left, right, TN, preferred_element_type=f32)
    following = 0.9 * momentum[0, 0] + grad[0, 0].astype(f32)
    momentum_next[0, 0] = following
    update[0] = delta
    error_next[0, 0] = (following + error[0, 0]) - delta


def finish(grad, error, momentum, unit, basis):
    block = 128
    rows = pl.BlockSpec((1, 1, block, COLS), lambda p, i: (0, p, i, 0))
    full = pl.BlockSpec((2, RANK, COLS), lambda p, i: (0, 0, 0))
    return pl.pallas_call(
        finish_kernel,
        grid=(2, ROWS // block),
        out_shape=(
            jax.ShapeDtypeStruct(error.shape, f32),
            jax.ShapeDtypeStruct(error.shape, f32),
            jax.ShapeDtypeStruct((2, ROWS, COLS), f32),
            jax.ShapeDtypeStruct((2, RANK, COLS), f32),
        ),
        in_specs=[rows, rows, rows, pl.BlockSpec((1, RANK, block), lambda p, i: (p, 0, i)), full],
        out_specs=(rows, rows, pl.BlockSpec((1, block, COLS), lambda p, i: (p, i, 0)), full),
        compiler_params=pltpu.CompilerParams(vmem_limit_bytes=32 * 2**20),
        name="update_and_error",
    )(grad, error, momentum, unit, basis)


def local(grad, error, momentum, warm_start):
    unit, basis = iterate(grad, error, momentum, jnp.swapaxes(warm_start, 1, 2))
    error_next, momentum_next, update, basis_next = finish(grad, error, momentum, unit, basis)
    return error_next, momentum_next, update, jnp.swapaxes(basis_next, 1, 2)


def solution(mesh):
    split = P("rep", None, "fsdp", None)
    return jax.shard_map(
        local, mesh=mesh, in_specs=(split, split, split, P()),
        out_specs=(split, split, P(None, "fsdp", None), P()), check_vma=False)
```

```python
import functools

import jax
import jax.numpy as jnp
from jax import lax
from jax.experimental import pallas as pl
from jax.experimental.pallas import tpu as pltpu
from jax.sharding import PartitionSpec as P

MESH = pl.DeviceIdType.MESH
f32 = jnp.float32
bf16 = jnp.bfloat16

RANK = 64
ROWS = 512
COLS = 1024
CHUNK = 128
CHUNKS = ROWS // CHUNK
CHIPS = 64
SELF = 42
NN = (((1,), (0,)), ((), ()))
NT = (((1,), (1,)), ((), ()))
TN = (((0,), (0,)), ((), ()))


def split3(x):
    high = x.astype(bf16)
    rest = x - high.astype(f32)
    mid = rest.astype(bf16)
    low = (rest - mid.astype(f32)).astype(bf16)
    return high, mid, low


def dot6(a, w, dims):
    n = a[0].shape[0]
    dot = functools.partial(lax.dot_general, dimension_numbers=dims, preferred_element_type=f32)
    s1 = dot(jnp.concatenate(a, axis=0), w[0])
    s2 = dot(jnp.concatenate(a[:2], axis=0), w[1])
    s3 = dot(a[0], w[2])
    return ((s1[2 * n:] + s2[n:]) + s3) + (s1[n:2 * n] + s2[:n]) + s1[:n]


def inverse_lower_factor(gram):
    n = RANK
    row_id = lax.broadcasted_iota(jnp.int32, (n, n), 0)
    col_id = lax.broadcasted_iota(jnp.int32, (n, n), 1)
    diagonal = row_id == col_id
    trace = jnp.sum(jnp.where(diagonal, gram, 0.0))
    a = jnp.concatenate(
        [gram + jnp.where(diagonal, 0.0001 * trace / n, 0.0), jnp.where(diagonal, 1.0, 0.0).astype(f32)], axis=1)
    rows = []
    for k in range(n):
        low = (k // 8) * 8
        a = a[low - (n - a.shape[0]):]
        at = k - low
        inv = lax.rsqrt(a[at:at + 1, k:k + 1])
        row = a[at:at + 1, :] * inv
        rows.append(row)
        col = a[:, k:k + 1] * inv
        below = lax.broadcasted_iota(jnp.int32, a.shape, 0) > at
        a = a - jnp.where(below, col * row, 0.0)
    return jnp.concatenate(rows, axis=0)[:, n:]


def iterate_kernel(grad, error, momentum, warm, merged_out, following_out, unit_out, basis_out,
                   g_buf, e_buf, m_buf, w_buf, landed, parts, across, warm_parts,
                   f_slots, y_tiles, y_terms, y_full, g_slots, mine_out, theirs_unit, theirs_basis,
                   load_sem, warm_sem, second, third, swap_send, swap_recv, f_send, f_recv, rs_send, rs_recv, ag_send, ag_recv,
                   gram_send, gram_recv, end_send, end_recv):
    rep = lax.axis_index("rep")
    fsdp = lax.axis_index("fsdp")
    z, core = rep // 2, lax.rem(rep, 2)
    x, y = fsdp // 4, lax.rem(fsdp, 4)
    chip = z * 16 + fsdp
    partner = (rep + 1 - 2 * core, fsdp)

    def load(role, q):
        p = core if role else 1 - core
        rows = pl.ds(q * CHUNK, CHUNK)
        return [
            pltpu.make_async_copy(ref.at[0, p, rows], buf.at[role, rows], load_sem.at[i, role, q])
            for i, (ref, buf) in enumerate(((grad, g_buf), (error, e_buf), (momentum, m_buf)))
        ]

    lines = [(lax.rem(z + d, 4) * 2 + core, fsdp) for d in (1, 2, 3)]
    lines += [(rep, lax.rem(x + d, 4) * 4 + y) for d in (1, 2, 3)]
    lines += [(rep, x * 4 + lax.rem(y + d, 4)) for d in (1, 2, 3)]

    def tell(sem):
        for device in lines:
            pl.semaphore_signal(sem, inc=1, device_id=device, device_id_type=MESH)

    barrier = pltpu.get_barrier_semaphore()
    tell(barrier)
    pl.semaphore_signal(barrier, inc=1, device_id=partner, device_id_type=MESH)

    warm_copy = pltpu.make_async_copy(warm.at[core], w_buf, warm_sem)
    for role in range(2):
        for q in range(CHUNKS):
            for copy in load(role, q):
                copy.start()
        if role == 0:
            warm_copy.start()

    def peer(k):
        pz = lax.rem(z + 2 + k // 16, 4)
        px = lax.rem(x + 2 + lax.rem(k // 4, 4), 4)
        py = lax.rem(y + 2 + lax.rem(k, 4), 4)
        return pz, px * 4 + py

    def each_peer(body):
        def step(k, carry):
            body(k)
            return carry
        lax.fori_loop(0, SELF, step, 0)
        lax.fori_loop(SELF + 1, CHIPS, step, 0)

    def swap(q):
        rows = pl.ds(q * CHUNK, CHUNK)
        return pltpu.make_async_remote_copy(
            src_ref=merged_out.at[1 - core, rows], dst_ref=landed.at[rows],
            send_sem=swap_send.at[q], recv_sem=swap_recv.at[q],
            device_id=partner, device_id_type=MESH)

    def merge(role, q):
        for copy in load(role, q):
            copy.wait()
        p = core if role else 1 - core
        rows = slice(q * CHUNK, (q + 1) * CHUNK)
        following = 0.9 * m_buf[role, rows] + g_buf[role, rows].astype(f32)
        following_out[p, rows] = following
        value = following + e_buf[role, rows]
        merged_out[p, rows] = value
        return value

    def f_copy(it, q, dz):
        block = f_slots.at[it, z, :, pl.ds(q * CHUNK, CHUNK)]
        pz = lax.rem(z + dz, 4)
        return pltpu.make_async_remote_copy(
            src_ref=block, dst_ref=block, send_sem=f_send.at[it, q, dz - 1], recv_sem=f_recv.at[it, q],
            device_id=(pz * 2 + core, fsdp), device_id_type=MESH)

    def f_all(it, q):
        three = f_slots.at[it, pl.ds(0, 3), :, pl.ds(q * CHUNK, CHUNK)]
        return pltpu.make_async_copy(three, three, f_recv.at[it, q])

    def send_factor(it, q, value):
        f_slots[it, z, :, q * CHUNK:(q + 1) * CHUNK] = value
        for dz in (2, 1, 3):
            f_copy(it, q, dz).start()

    for q in range(CHUNKS):
        merge(0, q)
        if q == 0:
            pl.semaphore_wait(barrier, 10)
        swap(q).start()
    tell(second)
    warm_copy.wait()
    for i, part in enumerate(split3(w_buf[...])):
        warm_parts[i] = part
    for q in range(CHUNKS):
        merge(1, q)
    pl.semaphore_wait(second, 9)
    tell(third)

    for q in range(CHUNKS):
        rows = slice(q * CHUNK, (q + 1) * CHUNK)
        swap(q).wait_recv()
        block = split3((merged_out[core, rows] + landed[rows]) * 0.125)
        for i in range(3):
            parts[i, rows] = block[i]
        send_factor(0, q, dot6([warm_parts[i] for i in range(3)], block, NT))

    def gram_copy(it, k):
        px = lax.rem(x + 2 + k // 4, 4)
        py = lax.rem(y + 2 + lax.rem(k, 4), 4)
        return pltpu.make_async_remote_copy(
            src_ref=g_slots.at[it, fsdp], dst_ref=g_slots.at[it, fsdp],
            send_sem=gram_send.at[it], recv_sem=gram_recv.at[it],
            device_id=(rep, px * 4 + py), device_id_type=MESH)

    def each_plane(body):
        def step(k, carry):
            body(k)
            return carry
        lax.fori_loop(0, 10, step, 0)
        lax.fori_loop(11, 16, step, 0)

    def rs_copy(it, k):
        pz, pf = peer(k)
        return pltpu.make_async_remote_copy(
            src_ref=y_tiles.at[it, pz * 16 + pf], dst_ref=y_terms.at[it, k],
            send_sem=rs_send.at[it], recv_sem=rs_recv.at[it], device_id=(pz * 2 + core, pf), device_id_type=MESH)

    def ag_copy(it, k):
        pz, pf = peer(k)
        return pltpu.make_async_remote_copy(
            src_ref=y_full.at[it, chip], dst_ref=y_full.at[it, chip],
            send_sem=ag_send.at[it], recv_sem=ag_recv.at[it], device_id=(pz * 2 + core, pf), device_id_type=MESH)

    def all_of(ref, sem):
        return pltpu.make_async_copy(ref, ref, sem)

    all_parts = lambda: [parts[i] for i in range(3)]
    for it in range(2):
        for q in range(CHUNKS):
            f_all(it, q).wait()
        factor = jnp.sum(f_slots[it], axis=0)
        factor_parts = split3(factor)
        gram = dot6(factor_parts, factor_parts, NT)
        g_slots[it, fsdp] = jnp.concatenate([gram[:32], gram[32:]], axis=1)
        if it == 0:
            pl.semaphore_wait(third, 9)
        each_plane(lambda k: gram_copy(it, k).start())

        term = dot6(factor_parts, all_parts(), NN)
        for a in range(8):
            for b in range(8):
                y_tiles[it, a * 8 + b] = term[a * 8:(a + 1) * 8, b * 128:(b + 1) * 128]
        y_terms[it, SELF] = y_tiles[it, chip]
        each_peer(lambda k: rs_copy(it, k).start())
        if it == 0:
            for i in range(3):
                across[i] = parts[i].T
        all_of(y_terms.at[it, pl.ds(0, CHIPS - 1)], rs_recv.at[it]).wait()
        y_full[it, chip] = jnp.sum(y_terms[it], axis=0)
        each_peer(lambda k: ag_copy(it, k).start())

        all_of(g_slots.at[it, pl.ds(0, 15)], gram_recv.at[it]).wait()
        packed = jnp.sum(g_slots[it], axis=0)
        inverse = inverse_lower_factor(jnp.concatenate([packed[:, :RANK], packed[:, RANK:]], axis=0))
        inverse_parts = split3(inverse)
        if it == 1:
            unit = dot6(inverse_parts, factor_parts, NN)
            unit_out[core] = unit
            mine_out[:, COLS:] = unit
            unit_copy = pltpu.make_async_remote_copy(
                src_ref=mine_out.at[:, pl.ds(COLS, ROWS)], dst_ref=theirs_unit,
                send_sem=end_send.at[0], recv_sem=end_recv.at[0], device_id=partner, device_id_type=MESH)
            unit_copy.start()

        all_of(y_full.at[it, pl.ds(0, CHIPS - 1)], ag_recv.at[it]).wait()
        total = jnp.concatenate(
            [jnp.concatenate([y_full[it, a * 8 + b] for b in range(8)], axis=1) for a in range(8)], axis=0)
        basis = dot6(inverse_parts, split3(total), NN)
        if it == 0:
            basis_parts = split3(basis)
            for q in range(CHUNKS):
                send_factor(1, q, dot6(basis_parts, [across[i, :, q * CHUNK:(q + 1) * CHUNK] for i in range(3)], NN))

    mine_out[:, :COLS] = basis
    basis_copy = pltpu.make_async_remote_copy(
        src_ref=mine_out.at[:, pl.ds(0, COLS)], dst_ref=theirs_basis,
        send_sem=end_send.at[1], recv_sem=end_recv.at[1], device_id=partner, device_id_type=MESH)
    basis_copy.start()
    basis_out[core] = basis
    unit_copy.wait_recv()
    unit_out[1 - core] = theirs_unit[...]

    for q in range(CHUNKS):
        swap(q).wait_send()
    for it in range(2):
        for q in range(CHUNKS):
            for dz in (1, 2, 3):
                f_copy(it, q, dz).wait_send()
        all_of(y_terms.at[it, pl.ds(0, CHIPS - 1)], rs_send.at[it]).wait()
        all_of(y_full.at[it, pl.ds(0, CHIPS - 1)], ag_send.at[it]).wait()
        all_of(g_slots.at[it, pl.ds(0, 15)], gram_send.at[it]).wait()
    unit_copy.wait_send()
    basis_copy.wait()
    basis_out[1 - core] = theirs_basis[...]


def iterate(grad, error, momentum, warm):
    vmem = pl.BlockSpec(memory_space=pltpu.VMEM)
    hbm = pl.BlockSpec(memory_space=pltpu.HBM)
    dma = pltpu.SemaphoreType.DMA
    return pl.pallas_call(
        iterate_kernel,
        out_shape=(
            jax.ShapeDtypeStruct((2, ROWS, COLS), f32), jax.ShapeDtypeStruct((2, ROWS, COLS), f32),
            jax.ShapeDtypeStruct((2, RANK, ROWS), f32), jax.ShapeDtypeStruct((2, RANK, COLS), f32)),
        in_specs=[hbm, hbm, hbm, hbm],
        out_specs=(vmem, vmem, vmem, vmem),
        scratch_shapes=[
            pltpu.VMEM((2, ROWS, COLS), bf16),
            pltpu.VMEM((2, ROWS, COLS), f32),
            pltpu.VMEM((2, ROWS, COLS), f32),
            pltpu.VMEM((RANK, COLS), f32),
            pltpu.VMEM((ROWS, COLS), f32),
            pltpu.VMEM((3, ROWS, COLS), bf16),
            pltpu.VMEM((3, COLS, ROWS), bf16),
            pltpu.VMEM((3, RANK, COLS), bf16),
            pltpu.VMEM((2, 4, RANK, ROWS), f32),
            pltpu.VMEM((2, CHIPS, 8, 128), f32),
            pltpu.VMEM((2, CHIPS, 8, 128), f32),
            pltpu.VMEM((2, CHIPS, 8, 128), f32),
            pltpu.VMEM((2, 16, 32, 128), f32),
            pltpu.VMEM((RANK, COLS + ROWS), f32),
            pltpu.VMEM((RANK, ROWS), f32),
            pltpu.VMEM((RANK, COLS), f32),
            dma((3, 2, CHUNKS)), dma,
            pltpu.SemaphoreType.REGULAR, pltpu.SemaphoreType.REGULAR,
            dma((CHUNKS,)), dma((CHUNKS,)),
            dma((2, CHUNKS, 3)), dma((2, CHUNKS)),
            dma((2,)), dma((2,)),
            dma((2,)), dma((2,)),
            dma((2,)), dma((2,)),
            dma((2,)), dma((2,)),
        ],
        compiler_params=pltpu.CompilerParams(
            collective_id=0, has_side_effects=True, vmem_limit_bytes=40 * 2**20),
        name="power_iterations",
    )(grad, error, momentum, warm)


BLOCK = 256


def finish_kernel(merged, following, unit, basis, error_next, momentum_next, update, basis_next,
                  delta_buf, error_buf, sems):
    steps = [(p, i) for p in range(2) for i in range(ROWS // BLOCK)]
    copies = [
        pltpu.make_async_copy(following, momentum_next.at[0], sems.at[0]),
        pltpu.make_async_copy(basis, basis_next, sems.at[1]),
    ]
    for copy in copies:
        copy.start()
    for n, (p, i) in enumerate(steps):
        rows = slice(i * BLOCK, (i + 1) * BLOCK)
        part = pl.ds(i * BLOCK, BLOCK)
        if i == 0:
            b = split3(basis[p])
            right = jnp.concatenate([b[0], b[1], b[0], b[2], b[0], b[1]], axis=0)
        u = split3(unit[p, :, rows])
        left = jnp.concatenate([u[0], u[0], u[1], u[0], u[2], u[1]], axis=0)
        delta = lax.dot_general(left, right, TN, preferred_element_type=f32)
        delta_buf[p, rows] = delta
        error_buf[p, rows] = merged[p, rows] - delta
        new = [
            pltpu.make_async_copy(delta_buf.at[p, part], update.at[p, part], sems.at[2 + 2 * n]),
            pltpu.make_async_copy(error_buf.at[p, part], error_next.at[0, p, part], sems.at[3 + 2 * n]),
        ]
        for copy in new:
            copy.start()
        copies += new
    for copy in copies:
        copy.wait()


def finish(merged, following, unit, basis):
    vmem = pl.BlockSpec(memory_space=pltpu.VMEM)
    hbm = pl.BlockSpec(memory_space=pltpu.HBM)
    whole = jax.ShapeDtypeStruct((1, 2, ROWS, COLS), f32)
    return pl.pallas_call(
        finish_kernel,
        out_shape=(whole, whole, jax.ShapeDtypeStruct((2, ROWS, COLS), f32), jax.ShapeDtypeStruct((2, RANK, COLS), f32)),
        in_specs=[vmem, vmem, vmem, vmem],
        out_specs=(hbm, hbm, hbm, hbm),
        scratch_shapes=[
            pltpu.VMEM((2, ROWS, COLS), f32), pltpu.VMEM((2, ROWS, COLS), f32),
            pltpu.SemaphoreType.DMA((2 + 4 * ROWS // BLOCK,))],
        compiler_params=pltpu.CompilerParams(vmem_limit_bytes=24 * 2**20),
        name="update_and_error",
    )(merged, following, unit, basis)


def local(grad, error, momentum, warm_start):
    merged, following, unit, basis = iterate(*(pltpu.with_memory_space_constraint(v, pltpu.HBM) for v in (grad, error, momentum, jnp.swapaxes(warm_start, 1, 2))))
    error_next, momentum_next, update, basis_next = finish(merged, following, unit, basis)
    return error_next, momentum_next, update, jnp.swapaxes(basis_next, 1, 2)


def solution(mesh):
    split = P("rep", None, "fsdp", None)
    return jax.shard_map(
        local, mesh=mesh, in_specs=(split, split, split, P()),
        out_specs=(split, split, P(None, "fsdp", None), P()), check_vma=False)
```

```python
import functools

import jax
import jax.numpy as jnp
from jax import lax
from jax.experimental import pallas as pl
from jax.experimental.pallas import tpu as pltpu
from jax.sharding import PartitionSpec as P

MESH = pl.DeviceIdType.MESH
f32 = jnp.float32
bf16 = jnp.bfloat16

RANK = 64
ROWS = 512
COLS = 1024
CHUNK = 128
CHUNKS = ROWS // CHUNK
CHIPS = 64
OFFSETS = sorted(
    ((dz, dx, dy) for dz in range(4) for dx in range(4) for dy in range(4) if dz or dx or dy),
    key=lambda o: -sum(min(d, 4 - d) for d in o))
PLANE = [o for o in OFFSETS if o[0] == 0]
NN = (((1,), (0,)), ((), ()))
NT = (((1,), (1,)), ((), ()))
TN = (((0,), (0,)), ((), ()))


def split3(x):
    high = x.astype(bf16)
    rest = x - high.astype(f32)
    mid = rest.astype(bf16)
    low = (rest - mid.astype(f32)).astype(bf16)
    return high, mid, low


def dot6(a, w, dims):
    n = a[0].shape[0]
    dot = functools.partial(lax.dot_general, dimension_numbers=dims, preferred_element_type=f32)
    s1 = dot(jnp.concatenate(a, axis=0), w[0])
    s2 = dot(jnp.concatenate(a[:2], axis=0), w[1])
    s3 = dot(a[0], w[2])
    return ((s1[2 * n:] + s2[n:]) + s3) + (s1[n:2 * n] + s2[:n]) + s1[:n]


def inverse_lower_factor(gram):
    n = RANK
    row_id = lax.broadcasted_iota(jnp.int32, (n, n), 0)
    col_id = lax.broadcasted_iota(jnp.int32, (n, n), 1)
    diagonal = row_id == col_id
    trace = jnp.sum(jnp.where(diagonal, gram, 0.0))
    a = jnp.concatenate(
        [gram + jnp.where(diagonal, 0.0001 * trace / n, 0.0), jnp.where(diagonal, 1.0, 0.0).astype(f32)], axis=1)
    done = []
    for k in range(0, n, 8):
        cols = [jnp.broadcast_to(a[:, k + j:k + j + 1], a.shape) for j in range(8)]
        rows = [a[j:j + 1, :] for j in range(8)]
        for j in range(8):
            inv = lax.rsqrt(cols[j][j:j + 1, :])
            rows[j] = rows[j] * inv
            cols[j] = cols[j] * inv
            for l in range(j + 1, 8):
                factor = cols[j][l:l + 1, :]
                rows[l] = rows[l] - factor * rows[j]
                cols[l] = cols[l] - factor * cols[j]
        done += rows
        a = a[8:]
        if k + 8 < n:
            for j in range(8):
                a = a - cols[j][8:] * rows[j]
    return jnp.concatenate(done, axis=0)[:, n:]


def iterate_kernel(grad, error, momentum, warm, merged_out, following_out, unit_out, basis_out,
                   g_buf, e_buf, m_buf, w_buf, landed, parts, across, warm_parts,
                   f_slots, y_tiles, y_terms, y_full, g_tiles, g_terms, g_full, theirs_unit, theirs_basis,
                   load_sem, warm_sem, second, third, swap_send, swap_recv, f_send, f_recv, rs_send, rs_recv, ag_send, ag_recv,
                   gram_send, gram_recv, gram_z_send, gram_z_recv, end_send, end_recv):
    rep = lax.axis_index("rep")
    fsdp = lax.axis_index("fsdp")
    z, core = rep // 2, lax.rem(rep, 2)
    x, y = fsdp // 4, lax.rem(fsdp, 4)
    chip = z * 16 + fsdp
    partner = (rep + 1 - 2 * core, fsdp)

    def load(role, q):
        p = core if role else 1 - core
        rows = pl.ds(q * CHUNK, CHUNK)
        return [
            pltpu.make_async_copy(ref.at[0, p, rows], buf.at[role, rows], load_sem.at[i, role, q])
            for i, (ref, buf) in enumerate(((grad, g_buf), (error, e_buf), (momentum, m_buf)))
        ]

    zs = [lax.rem(z + d, 4) for d in range(4)]
    xs = [lax.rem(x + d, 4) for d in range(4)]
    ys = [lax.rem(y + d, 4) for d in range(4)]
    lines = [(zs[d] * 2 + core, fsdp) for d in (1, 2, 3)]
    lines += [(rep, xs[d] * 4 + y) for d in (1, 2, 3)]
    lines += [(rep, x * 4 + ys[d]) for d in (1, 2, 3)]

    def tell(sem):
        for device in lines:
            pl.semaphore_signal(sem, inc=1, device_id=device, device_id_type=MESH)

    barrier = pltpu.get_barrier_semaphore()
    tell(barrier)
    pl.semaphore_signal(barrier, inc=1, device_id=partner, device_id_type=MESH)

    warm_copy = pltpu.make_async_copy(warm.at[core], w_buf, warm_sem)
    for role in range(2):
        for q in range(CHUNKS):
            for copy in load(role, q):
                copy.start()
        if role == 0:
            warm_copy.start()

    def chip_at(offset):
        dz, dx, dy = offset
        return zs[dz], xs[dx] * 4 + ys[dy]

    def swap(q):
        rows = pl.ds(q * CHUNK, CHUNK)
        return pltpu.make_async_remote_copy(
            src_ref=merged_out.at[1 - core, rows], dst_ref=landed.at[rows],
            send_sem=swap_send.at[q], recv_sem=swap_recv.at[q],
            device_id=partner, device_id_type=MESH)

    def merge(role, q):
        for copy in load(role, q):
            copy.wait()
        p = core if role else 1 - core
        rows = slice(q * CHUNK, (q + 1) * CHUNK)
        following = 0.9 * m_buf[role, rows] + g_buf[role, rows].astype(f32)
        following_out[p, rows] = following
        value = following + e_buf[role, rows]
        merged_out[p, rows] = value
        return value

    def f_copy(it, q, dz):
        block = f_slots.at[it, z, :, pl.ds(q * CHUNK, CHUNK)]
        return pltpu.make_async_remote_copy(
            src_ref=block, dst_ref=block, send_sem=f_send.at[it, q, dz - 1], recv_sem=f_recv.at[it, q],
            device_id=(zs[dz] * 2 + core, fsdp), device_id_type=MESH)

    def f_all(it, q):
        three = f_slots.at[it, pl.ds(0, 3), :, pl.ds(q * CHUNK, CHUNK)]
        return pltpu.make_async_copy(three, three, f_recv.at[it, q])

    def send_factor(it, q, value):
        f_slots[it, z, :, q * CHUNK:(q + 1) * CHUNK] = value
        for dz in (2, 1, 3):
            f_copy(it, q, dz).start()

    for q in range(CHUNKS):
        merge(0, q)
        if q == 0:
            pl.semaphore_wait(barrier, 10)
        swap(q).start()
        if q == 0:
            tell(second)
    warm_copy.wait()
    for i, part in enumerate(split3(w_buf[...])):
        warm_parts[i] = part

    for q in range(CHUNKS):
        rows = slice(q * CHUNK, (q + 1) * CHUNK)
        own = merge(1, q)
        swap(q).wait_recv()
        block = split3((own + landed[rows]) * 0.125)
        for i in range(3):
            parts[i, rows] = block[i]
        send_factor(0, q, dot6([warm_parts[i] for i in range(3)], block, NT))
        if q == 1:
            pl.semaphore_wait(second, 9)
            tell(third)

    def gram_copy(it, offset):
        _, pf = chip_at(offset)
        return pltpu.make_async_remote_copy(
            src_ref=g_tiles.at[it, z], dst_ref=g_terms.at[it, fsdp],
            send_sem=gram_send.at[it], recv_sem=gram_recv.at[it],
            device_id=(rep, pf), device_id_type=MESH)

    def gram_z_copy(it, dz):
        return pltpu.make_async_remote_copy(
            src_ref=g_full.at[it, z], dst_ref=g_full.at[it, z],
            send_sem=gram_z_send.at[it], recv_sem=gram_z_recv.at[it],
            device_id=(zs[dz] * 2 + core, fsdp), device_id_type=MESH)

    def rs_copy(it, k):
        pz, pf = chip_at(OFFSETS[k])
        return pltpu.make_async_remote_copy(
            src_ref=y_tiles.at[it, pz * 16 + pf], dst_ref=y_terms.at[it, k],
            send_sem=rs_send.at[it], recv_sem=rs_recv.at[it], device_id=(pz * 2 + core, pf), device_id_type=MESH)

    def ag_copy(it, k):
        pz, pf = chip_at(OFFSETS[k])
        return pltpu.make_async_remote_copy(
            src_ref=y_full.at[it, chip], dst_ref=y_full.at[it, chip],
            send_sem=ag_send.at[it], recv_sem=ag_recv.at[it], device_id=(pz * 2 + core, pf), device_id_type=MESH)

    def all_of(ref, sem):
        return pltpu.make_async_copy(ref, ref, sem)

    def basis_copy(half):
        part = pl.ds(half * (COLS // 2), COLS // 2)
        return pltpu.make_async_remote_copy(
            src_ref=basis_out.at[core, :, part], dst_ref=theirs_basis.at[:, part],
            send_sem=end_send.at[half], recv_sem=end_recv.at[half], device_id=partner, device_id_type=MESH)

    unit_copy = pltpu.make_async_remote_copy(
        src_ref=unit_out.at[core], dst_ref=theirs_unit,
        send_sem=end_send.at[2], recv_sem=end_recv.at[2], device_id=partner, device_id_type=MESH)

    for it in range(2):
        pieces = []
        term = None
        for q in range(CHUNKS):
            f_all(it, q).wait()
            piece = split3(jnp.sum(f_slots[it, :, :, q * CHUNK:(q + 1) * CHUNK], axis=0))
            pieces.append(piece)
            more = dot6(piece, [parts[i, q * CHUNK:(q + 1) * CHUNK] for i in range(3)], NN)
            term = more if q == 0 else term + more
        for a in range(8):
            for b in range(8):
                y_tiles[it, a * 8 + b] = term[a * 8:(a + 1) * 8, b * 128:(b + 1) * 128]
        y_terms[it, CHIPS - 1] = y_tiles[it, chip]
        if it == 0:
            pl.semaphore_wait(third, 9)
        for k in range(CHIPS - 1):
            rs_copy(it, k).start()

        factor_parts = tuple(jnp.concatenate([piece[i] for piece in pieces], axis=1) for i in range(3))
        gram = dot6(factor_parts, factor_parts, NT)
        packed = jnp.concatenate([gram[:32], gram[32:]], axis=1)
        for i in range(4):
            g_tiles[it, i] = packed[i * 8:(i + 1) * 8]
        g_terms[it, fsdp] = g_tiles[it, z]
        for offset in PLANE:
            gram_copy(it, offset).start()
        if it == 0:
            for i in range(3):
                across[i] = parts[i].T

        all_of(y_terms.at[it, pl.ds(0, CHIPS - 1)], rs_recv.at[it]).wait()
        y_full[it, chip] = sum(jnp.sum(y_terms[it, i * 16:(i + 1) * 16], axis=0) for i in range(4))
        for k in range(CHIPS - 1):
            ag_copy(it, k).start()

        all_of(g_terms.at[it, pl.ds(0, 15)], gram_recv.at[it]).wait()
        g_full[it, z] = jnp.sum(g_terms[it], axis=0)
        for dz in (2, 1, 3):
            gram_z_copy(it, dz).start()
        all_of(g_full.at[it, pl.ds(0, 3)], gram_z_recv.at[it]).wait()
        packed = jnp.concatenate([g_full[it, i] for i in range(4)], axis=0)
        inverse = inverse_lower_factor(jnp.concatenate([packed[:, :RANK], packed[:, RANK:]], axis=0))
        inverse_parts = split3(inverse)
        if it == 1:
            unit_out[core] = dot6(inverse_parts, factor_parts, NN)
            unit_copy.start()

        all_of(y_full.at[it, pl.ds(0, CHIPS - 1)], ag_recv.at[it]).wait()
        total = split3(jnp.concatenate(
            [jnp.concatenate([y_full[it, a * 8 + b] for b in range(8)], axis=1) for a in range(8)], axis=0))
        if it == 0:
            basis_parts = split3(dot6(inverse_parts, total, NN))
            for q in range(CHUNKS):
                send_factor(1, q, dot6(basis_parts, [across[i, :, q * CHUNK:(q + 1) * CHUNK] for i in range(3)], NN))

    for half in range(2):
        part = slice(half * (COLS // 2), (half + 1) * (COLS // 2))
        basis_out[core, :, part] = dot6(inverse_parts, [v[:, part] for v in total], NN)
        basis_copy(half).start()
    unit_copy.wait_recv()
    unit_out[1 - core] = theirs_unit[...]

    for q in range(CHUNKS):
        swap(q).wait_send()
    for it in range(2):
        for q in range(CHUNKS):
            for dz in (1, 2, 3):
                f_copy(it, q, dz).wait_send()
        all_of(y_terms.at[it, pl.ds(0, CHIPS - 1)], rs_send.at[it]).wait()
        all_of(y_full.at[it, pl.ds(0, CHIPS - 1)], ag_send.at[it]).wait()
        all_of(g_terms.at[it, pl.ds(0, 15)], gram_send.at[it]).wait()
        all_of(g_full.at[it, pl.ds(0, 3)], gram_z_send.at[it]).wait()
    unit_copy.wait_send()
    for half in range(2):
        basis_copy(half).wait()
    basis_out[1 - core] = theirs_basis[...]


def iterate(grad, error, momentum, warm):
    vmem = pl.BlockSpec(memory_space=pltpu.VMEM)
    hbm = pl.BlockSpec(memory_space=pltpu.HBM)
    dma = pltpu.SemaphoreType.DMA
    return pl.pallas_call(
        iterate_kernel,
        out_shape=(
            jax.ShapeDtypeStruct((2, ROWS, COLS), f32), jax.ShapeDtypeStruct((2, ROWS, COLS), f32),
            jax.ShapeDtypeStruct((2, RANK, ROWS), f32), jax.ShapeDtypeStruct((2, RANK, COLS), f32)),
        in_specs=[hbm, hbm, hbm, hbm],
        out_specs=(vmem, vmem, vmem, vmem),
        scratch_shapes=[
            pltpu.VMEM((2, ROWS, COLS), bf16),
            pltpu.VMEM((2, ROWS, COLS), f32),
            pltpu.VMEM((2, ROWS, COLS), f32),
            pltpu.VMEM((RANK, COLS), f32),
            pltpu.VMEM((ROWS, COLS), f32),
            pltpu.VMEM((3, ROWS, COLS), bf16),
            pltpu.VMEM((3, COLS, ROWS), bf16),
            pltpu.VMEM((3, RANK, COLS), bf16),
            pltpu.VMEM((2, 4, RANK, ROWS), f32),
            pltpu.VMEM((2, CHIPS, 8, 128), f32),
            pltpu.VMEM((2, CHIPS, 8, 128), f32),
            pltpu.VMEM((2, CHIPS, 8, 128), f32),
            pltpu.VMEM((2, 4, 8, 128), f32),
            pltpu.VMEM((2, 16, 8, 128), f32),
            pltpu.VMEM((2, 4, 8, 128), f32),
            pltpu.VMEM((RANK, ROWS), f32),
            pltpu.VMEM((RANK, COLS), f32),
            dma((3, 2, CHUNKS)), dma,
            pltpu.SemaphoreType.REGULAR, pltpu.SemaphoreType.REGULAR,
            dma((CHUNKS,)), dma((CHUNKS,)),
            dma((2, CHUNKS, 3)), dma((2, CHUNKS)),
            dma((2,)), dma((2,)),
            dma((2,)), dma((2,)),
            dma((2,)), dma((2,)),
            dma((2,)), dma((2,)),
            dma((3,)), dma((3,)),
        ],
        compiler_params=pltpu.CompilerParams(
            collective_id=0, has_side_effects=True, vmem_limit_bytes=40 * 2**20),
        name="power_iterations",
    )(grad, error, momentum, warm)


BLOCK = 256


def finish_kernel(merged, following, unit, basis, error_next, momentum_next, update, basis_next,
                  delta_buf, error_buf, sems):
    steps = [(p, i) for p in range(2) for i in range(ROWS // BLOCK)]
    copies = [
        pltpu.make_async_copy(following, momentum_next.at[0], sems.at[0]),
        pltpu.make_async_copy(basis, basis_next, sems.at[1]),
    ]
    for copy in copies:
        copy.start()
    for n, (p, i) in enumerate(steps):
        rows = slice(i * BLOCK, (i + 1) * BLOCK)
        part = pl.ds(i * BLOCK, BLOCK)
        if i == 0:
            b = split3(basis[p])
            right = jnp.concatenate([b[0], b[1], b[0], b[2], b[0], b[1]], axis=0)
        u = split3(unit[p, :, rows])
        left = jnp.concatenate([u[0], u[0], u[1], u[0], u[2], u[1]], axis=0)
        delta = lax.dot_general(left, right, TN, preferred_element_type=f32)
        delta_buf[p, rows] = delta
        error_buf[p, rows] = merged[p, rows] - delta
        new = [
            pltpu.make_async_copy(delta_buf.at[p, part], update.at[p, part], sems.at[2 + 2 * n]),
            pltpu.make_async_copy(error_buf.at[p, part], error_next.at[0, p, part], sems.at[3 + 2 * n]),
        ]
        for copy in new:
            copy.start()
        copies += new
    for copy in copies:
        copy.wait()


def finish(merged, following, unit, basis):
    vmem = pl.BlockSpec(memory_space=pltpu.VMEM)
    hbm = pl.BlockSpec(memory_space=pltpu.HBM)
    whole = jax.ShapeDtypeStruct((1, 2, ROWS, COLS), f32)
    return pl.pallas_call(
        finish_kernel,
        out_shape=(whole, whole, jax.ShapeDtypeStruct((2, ROWS, COLS), f32), jax.ShapeDtypeStruct((2, RANK, COLS), f32)),
        in_specs=[vmem, vmem, vmem, vmem],
        out_specs=(hbm, hbm, hbm, hbm),
        scratch_shapes=[
            pltpu.VMEM((2, ROWS, COLS), f32), pltpu.VMEM((2, ROWS, COLS), f32),
            pltpu.SemaphoreType.DMA((2 + 4 * ROWS // BLOCK,))],
        compiler_params=pltpu.CompilerParams(vmem_limit_bytes=24 * 2**20),
        name="update_and_error",
    )(merged, following, unit, basis)


def local(grad, error, momentum, warm_start):
    merged, following, unit, basis = iterate(*(pltpu.with_memory_space_constraint(v, pltpu.HBM) for v in (grad, error, momentum, jnp.swapaxes(warm_start, 1, 2))))
    error_next, momentum_next, update, basis_next = finish(merged, following, unit, basis)
    return error_next, momentum_next, update, jnp.swapaxes(basis_next, 1, 2)


def solution(mesh):
    split = P("rep", None, "fsdp", None)
    return jax.shard_map(
        local, mesh=mesh, in_specs=(split, split, split, P()),
        out_specs=(split, split, P(None, "fsdp", None), P()), check_vma=False)
```

```python
import functools

import jax
import jax.numpy as jnp
from jax import lax
from jax.experimental import pallas as pl
from jax.experimental.pallas import tpu as pltpu
from jax.sharding import PartitionSpec as P

MESH = pl.DeviceIdType.MESH
f32 = jnp.float32
bf16 = jnp.bfloat16

RANK = 64
ROWS = 512
COLS = 1024
CHUNK = 128
CHUNKS = ROWS // CHUNK
CHIPS = 64
OFFSETS = sorted(
    ((dz, dx, dy) for dz in range(4) for dx in range(4) for dy in range(4) if dz or dx or dy),
    key=lambda o: -sum(min(d, 4 - d) for d in o))
PLANE = [o for o in OFFSETS if o[0] == 0]
NN = (((1,), (0,)), ((), ()))
NT = (((1,), (1,)), ((), ()))
TN = (((0,), (0,)), ((), ()))


def split3(x):
    high = x.astype(bf16)
    rest = x - high.astype(f32)
    mid = rest.astype(bf16)
    low = (rest - mid.astype(f32)).astype(bf16)
    return high, mid, low


def whole(tiles):
    return jnp.concatenate(
        [jnp.concatenate([tiles[a * 8 + b] for b in range(8)], axis=1) for a in range(8)], axis=0)


def dot6(a, w, dims):
    n = a[0].shape[0]
    dot = functools.partial(lax.dot_general, dimension_numbers=dims, preferred_element_type=f32)
    s1 = dot(jnp.concatenate(a, axis=0), w[0])
    s2 = dot(jnp.concatenate(a[:2], axis=0), w[1])
    s3 = dot(a[0], w[2])
    return ((s1[2 * n:] + s2[n:]) + s3) + (s1[n:2 * n] + s2[:n]) + s1[:n]


def inverse_lower_factor(gram):
    n = RANK
    row_id = lax.broadcasted_iota(jnp.int32, (n, n), 0)
    col_id = lax.broadcasted_iota(jnp.int32, (n, n), 1)
    diagonal = row_id == col_id
    trace = jnp.sum(jnp.where(diagonal, gram, 0.0))
    a = jnp.concatenate(
        [gram + jnp.where(diagonal, 0.0001 * trace / n, 0.0), jnp.where(diagonal, 1.0, 0.0).astype(f32)], axis=1)
    done = []
    for k in range(0, n, 8):
        cols = [jnp.broadcast_to(a[:, k + j:k + j + 1], a.shape) for j in range(8)]
        rows = [a[j:j + 1, :] for j in range(8)]
        for j in range(8):
            inv = lax.rsqrt(cols[j][j:j + 1, :])
            rows[j] = rows[j] * inv
            cols[j] = cols[j] * inv
            for l in range(j + 1, 8):
                factor = cols[j][l:l + 1, :]
                rows[l] = rows[l] - factor * rows[j]
                cols[l] = cols[l] - factor * cols[j]
        done += rows
        a = a[8:]
        if k + 8 < n:
            for j in range(8):
                a = a - cols[j][8:] * rows[j]
    return jnp.concatenate(done, axis=0)[:, n:]


def iterate_kernel(grad, error, momentum, warm, merged_out, following_out, side_out, right_out,
                   g_buf, e_buf, m_buf, w_buf, landed, parts, across, warm_parts,
                   f_slots, y_tiles, y_terms, y_full, g_tiles, g_terms, g_full, theirs_side, theirs_right,
                   load_sem, warm_sem, second, third, swap_send, swap_recv, f_send, f_recv, rs_send, rs_recv, ag_send, ag_recv,
                   gram_send, gram_recv, gram_z_send, gram_z_recv, end_send, end_recv):
    rep = lax.axis_index("rep")
    fsdp = lax.axis_index("fsdp")
    z, core = rep // 2, lax.rem(rep, 2)
    x, y = fsdp // 4, lax.rem(fsdp, 4)
    chip = z * 16 + fsdp
    partner = (rep + 1 - 2 * core, fsdp)

    def load(role, q):
        p = core if role else 1 - core
        rows = pl.ds(q * CHUNK, CHUNK)
        return [
            pltpu.make_async_copy(ref.at[0, p, rows], buf.at[role, rows], load_sem.at[i, role, q])
            for i, (ref, buf) in enumerate(((grad, g_buf), (error, e_buf), (momentum, m_buf)))
        ]

    zs = [lax.rem(z + d, 4) for d in range(4)]
    xs = [lax.rem(x + d, 4) for d in range(4)]
    ys = [lax.rem(y + d, 4) for d in range(4)]
    lines = [(zs[d] * 2 + core, fsdp) for d in (1, 2, 3)]
    lines += [(rep, xs[d] * 4 + y) for d in (1, 2, 3)]
    lines += [(rep, x * 4 + ys[d]) for d in (1, 2, 3)]

    def tell(sem):
        for device in lines:
            pl.semaphore_signal(sem, inc=1, device_id=device, device_id_type=MESH)

    barrier = pltpu.get_barrier_semaphore()
    tell(barrier)
    pl.semaphore_signal(barrier, inc=1, device_id=partner, device_id_type=MESH)

    warm_copy = pltpu.make_async_copy(warm.at[core], w_buf, warm_sem)
    for role in range(2):
        for q in range(CHUNKS):
            for copy in load(role, q):
                copy.start()
        if role == 0:
            warm_copy.start()

    def chip_at(offset):
        dz, dx, dy = offset
        return zs[dz], xs[dx] * 4 + ys[dy]

    def swap(q):
        rows = pl.ds(q * CHUNK, CHUNK)
        return pltpu.make_async_remote_copy(
            src_ref=merged_out.at[1 - core, rows], dst_ref=landed.at[rows],
            send_sem=swap_send.at[q], recv_sem=swap_recv.at[q],
            device_id=partner, device_id_type=MESH)

    def merge(role, q):
        for copy in load(role, q):
            copy.wait()
        p = core if role else 1 - core
        rows = slice(q * CHUNK, (q + 1) * CHUNK)
        following = 0.9 * m_buf[role, rows] + g_buf[role, rows].astype(f32)
        following_out[p, rows] = following
        value = following + e_buf[role, rows]
        merged_out[p, rows] = value
        return value

    def f_copy(it, q, dz):
        block = f_slots.at[it, q, z]
        return pltpu.make_async_remote_copy(
            src_ref=block, dst_ref=block, send_sem=f_send.at[it, q, dz - 1], recv_sem=f_recv.at[it, q],
            device_id=(zs[dz] * 2 + core, fsdp), device_id_type=MESH)

    def f_all(it, q):
        three = f_slots.at[it, q, pl.ds(0, 3)]
        return pltpu.make_async_copy(three, three, f_recv.at[it, q])

    def send_factor(it, q, value):
        f_slots[it, q, z] = value
        for dz in (2, 1, 3):
            f_copy(it, q, dz).start()

    for q in range(CHUNKS):
        merge(0, q)
        if q == 0:
            pl.semaphore_wait(barrier, 10)
        swap(q).start()
        if q == 0:
            tell(second)
    warm_copy.wait()
    for i, part in enumerate(split3(w_buf[...])):
        warm_parts[i] = part

    for q in range(CHUNKS):
        rows = slice(q * CHUNK, (q + 1) * CHUNK)
        own = merge(1, q)
        swap(q).wait_recv()
        block = split3((own + landed[rows]) * 0.125)
        for i in range(3):
            parts[i, rows] = block[i]
        send_factor(0, q, dot6([warm_parts[i] for i in range(3)], block, NT))
        if q == 1:
            pl.semaphore_wait(second, 9)
            tell(third)

    def gram_copy(it, offset):
        _, pf = chip_at(offset)
        return pltpu.make_async_remote_copy(
            src_ref=g_tiles.at[it, z], dst_ref=g_terms.at[it, fsdp],
            send_sem=gram_send.at[it], recv_sem=gram_recv.at[it],
            device_id=(rep, pf), device_id_type=MESH)

    def gram_z_copy(it, dz):
        return pltpu.make_async_remote_copy(
            src_ref=g_full.at[it, z], dst_ref=g_full.at[it, z],
            send_sem=gram_z_send.at[it], recv_sem=gram_z_recv.at[it],
            device_id=(zs[dz] * 2 + core, fsdp), device_id_type=MESH)

    def rs_copy(it, k):
        pz, pf = chip_at(OFFSETS[k])
        return pltpu.make_async_remote_copy(
            src_ref=y_tiles.at[it, pz * 16 + pf], dst_ref=y_terms.at[it, k],
            send_sem=rs_send.at[it], recv_sem=rs_recv.at[it], device_id=(pz * 2 + core, pf), device_id_type=MESH)

    def ag_copy(it, k):
        pz, pf = chip_at(OFFSETS[k])
        return pltpu.make_async_remote_copy(
            src_ref=y_full.at[it, chip], dst_ref=y_full.at[it, chip],
            send_sem=ag_send.at[it], recv_sem=ag_recv.at[it, OFFSETS[k][0]], device_id=(pz * 2 + core, pf), device_id_type=MESH)

    def all_of(ref, sem):
        return pltpu.make_async_copy(ref, ref, sem)

    def gathered(it, d):
        return all_of(y_full.at[it, pl.ds(0, 16 if d else 15)], ag_recv.at[it, d])

    def right_copy(d):
        part = pl.ds(zs[(4 - d) % 4] * 16, 16)
        return pltpu.make_async_remote_copy(
            src_ref=y_full.at[1, part], dst_ref=theirs_right.at[part],
            send_sem=end_send.at[d], recv_sem=end_recv.at[d], device_id=partner, device_id_type=MESH)

    side_copy = pltpu.make_async_remote_copy(
        src_ref=side_out.at[core], dst_ref=theirs_side,
        send_sem=end_send.at[4], recv_sem=end_recv.at[4], device_id=partner, device_id_type=MESH)

    for it in range(2):
        pieces = []
        term = None
        for q in range(CHUNKS):
            f_all(it, q).wait()
            piece = split3(jnp.sum(f_slots[it, q], axis=0))
            pieces.append(piece)
            more = dot6(piece, [parts[i, q * CHUNK:(q + 1) * CHUNK] for i in range(3)], NN)
            term = more if q == 0 else term + more
            if q < CHUNKS - 1:
                square = dot6(piece, piece, NT)
                gram = square if q == 0 else gram + square
        for a in range(8):
            for b in range(8):
                y_tiles[it, a * 8 + b] = term[a * 8:(a + 1) * 8, b * 128:(b + 1) * 128]
        y_terms[it, CHIPS - 1] = y_tiles[it, chip]
        if it == 0:
            pl.semaphore_wait(third, 9)
        for k in range(CHIPS - 1):
            rs_copy(it, k).start()

        factor_parts = tuple(jnp.concatenate([piece[i] for piece in pieces], axis=1) for i in range(3))
        gram = gram + dot6(piece, piece, NT)
        packed = jnp.concatenate([gram[:32], gram[32:]], axis=1)
        for i in range(4):
            g_tiles[it, i] = packed[i * 8:(i + 1) * 8]
        g_terms[it, fsdp] = g_tiles[it, z]
        for offset in PLANE:
            gram_copy(it, offset).start()
        if it == 0:
            for i in range(3):
                across[i] = parts[i].T

        all_of(g_terms.at[it, pl.ds(0, 15)], gram_recv.at[it]).wait()
        g_full[it, z] = jnp.sum(g_terms[it], axis=0)
        for dz in (2, 1, 3):
            gram_z_copy(it, dz).start()

        all_of(y_terms.at[it, pl.ds(0, CHIPS - 1)], rs_recv.at[it]).wait()
        y_full[it, chip] = sum(jnp.sum(y_terms[it, i * 16:(i + 1) * 16], axis=0) for i in range(4))
        for k in range(CHIPS - 1):
            ag_copy(it, k).start()

        all_of(g_full.at[it, pl.ds(0, 3)], gram_z_recv.at[it]).wait()
        packed = jnp.concatenate([g_full[it, i] for i in range(4)], axis=0)
        inverse = inverse_lower_factor(jnp.concatenate([packed[:, :RANK], packed[:, RANK:]], axis=0))
        inverse_parts = split3(inverse)
        if it == 1:
            side_out[core, :, :ROWS] = dot6(inverse_parts, factor_parts, NN)
            side_out[core, :, ROWS:] = jnp.concatenate([inverse, jnp.zeros_like(inverse)], axis=1)
            side_copy.start()

        for d in (0, 1, 3, 2):
            gathered(it, d).wait()
            if it == 1:
                right_copy(d).start()
        if it == 0:
            total = split3(whole(y_full[0]))
            for h in range(0, CHUNKS, 2):
                wide = dot6(total, [across[i, :, h * CHUNK:(h + 2) * CHUNK] for i in range(3)], NN)
                wide = dot6(inverse_parts, split3(wide), NN)
                send_factor(1, h, wide[:, :CHUNK])
                send_factor(1, h + 1, wide[:, CHUNK:])

    right_out[core] = y_full[1]
    side_copy.wait()
    side_out[1 - core] = theirs_side[...]
    for q in range(CHUNKS):
        swap(q).wait_send()
    for it in range(2):
        for q in range(CHUNKS):
            for dz in (1, 2, 3):
                f_copy(it, q, dz).wait_send()
        all_of(y_terms.at[it, pl.ds(0, CHIPS - 1)], rs_send.at[it]).wait()
        all_of(y_full.at[it, pl.ds(0, CHIPS - 1)], ag_send.at[it]).wait()
        all_of(g_terms.at[it, pl.ds(0, 15)], gram_send.at[it]).wait()
        all_of(g_full.at[it, pl.ds(0, 3)], gram_z_send.at[it]).wait()
    for d in (0, 1, 3, 2):
        right_copy(d).wait()
    right_out[1 - core] = theirs_right[...]


def iterate(grad, error, momentum, warm):
    vmem = pl.BlockSpec(memory_space=pltpu.VMEM)
    hbm = pl.BlockSpec(memory_space=pltpu.HBM)
    dma = pltpu.SemaphoreType.DMA
    return pl.pallas_call(
        iterate_kernel,
        out_shape=(
            jax.ShapeDtypeStruct((2, ROWS, COLS), f32), jax.ShapeDtypeStruct((2, ROWS, COLS), f32),
            jax.ShapeDtypeStruct((2, RANK, ROWS + 128), f32), jax.ShapeDtypeStruct((2, CHIPS, 8, 128), f32)),
        in_specs=[hbm, hbm, hbm, hbm],
        out_specs=(vmem, vmem, vmem, vmem),
        scratch_shapes=[
            pltpu.VMEM((2, ROWS, COLS), bf16),
            pltpu.VMEM((2, ROWS, COLS), f32),
            pltpu.VMEM((2, ROWS, COLS), f32),
            pltpu.VMEM((RANK, COLS), f32),
            pltpu.VMEM((ROWS, COLS), f32),
            pltpu.VMEM((3, ROWS, COLS), bf16),
            pltpu.VMEM((3, COLS, ROWS), bf16),
            pltpu.VMEM((3, RANK, COLS), bf16),
            pltpu.VMEM((2, CHUNKS, 4, RANK, CHUNK), f32),
            pltpu.VMEM((2, CHIPS, 8, 128), f32),
            pltpu.VMEM((2, CHIPS, 8, 128), f32),
            pltpu.VMEM((2, CHIPS, 8, 128), f32),
            pltpu.VMEM((2, 4, 8, 128), f32),
            pltpu.VMEM((2, 16, 8, 128), f32),
            pltpu.VMEM((2, 4, 8, 128), f32),
            pltpu.VMEM((RANK, ROWS + 128), f32),
            pltpu.VMEM((CHIPS, 8, 128), f32),
            dma((3, 2, CHUNKS)), dma,
            pltpu.SemaphoreType.REGULAR, pltpu.SemaphoreType.REGULAR,
            dma((CHUNKS,)), dma((CHUNKS,)),
            dma((2, CHUNKS, 3)), dma((2, CHUNKS)),
            dma((2,)), dma((2,)),
            dma((2,)), dma((2, 4)),
            dma((2,)), dma((2,)),
            dma((2,)), dma((2,)),
            dma((5,)), dma((5,)),
        ],
        compiler_params=pltpu.CompilerParams(
            collective_id=0, has_side_effects=True, vmem_limit_bytes=40 * 2**20),
        name="power_iterations",
    )(grad, error, momentum, warm)


BLOCK = 256


def finish_kernel(merged, following, side, right_tiles, error_next, momentum_next, update, basis_next,
                  basis, delta_buf, error_buf, sems):
    steps = [(p, i) for p in range(2) for i in range(ROWS // BLOCK)]
    copies = [
        pltpu.make_async_copy(following, momentum_next.at[0], sems.at[0]),
        pltpu.make_async_copy(basis, basis_next, sems.at[1]),
    ]
    copies[0].start()
    for n, (p, i) in enumerate(steps):
        rows = slice(i * BLOCK, (i + 1) * BLOCK)
        part = pl.ds(i * BLOCK, BLOCK)
        if i == 0:
            inverse = split3(side[p, :, ROWS:ROWS + RANK])
            value = dot6(inverse, split3(whole(right_tiles[p])), NN)
            basis[p] = value
            b = split3(value)
            right = jnp.concatenate([b[0], b[1], b[0], b[2], b[0], b[1]], axis=0)
        u = split3(side[p, :, rows])
        left = jnp.concatenate([u[0], u[0], u[1], u[0], u[2], u[1]], axis=0)
        delta = lax.dot_general(left, right, TN, preferred_element_type=f32)
        delta_buf[p, rows] = delta
        error_buf[p, rows] = merged[p, rows] - delta
        new = [
            pltpu.make_async_copy(delta_buf.at[p, part], update.at[p, part], sems.at[2 + 2 * n]),
            pltpu.make_async_copy(error_buf.at[p, part], error_next.at[0, p, part], sems.at[3 + 2 * n]),
        ]
        for copy in new:
            copy.start()
        copies += new
    copies[1].start()
    for copy in copies:
        copy.wait()


def finish(merged, following, side, right_tiles):
    vmem = pl.BlockSpec(memory_space=pltpu.VMEM)
    hbm = pl.BlockSpec(memory_space=pltpu.HBM)
    kept = jax.ShapeDtypeStruct((1, 2, ROWS, COLS), f32)
    return pl.pallas_call(
        finish_kernel,
        out_shape=(kept, kept, jax.ShapeDtypeStruct((2, ROWS, COLS), f32), jax.ShapeDtypeStruct((2, RANK, COLS), f32)),
        in_specs=[vmem, vmem, vmem, vmem],
        out_specs=(hbm, hbm, hbm, hbm),
        scratch_shapes=[
            pltpu.VMEM((2, RANK, COLS), f32),
            pltpu.VMEM((2, ROWS, COLS), f32), pltpu.VMEM((2, ROWS, COLS), f32),
            pltpu.SemaphoreType.DMA((2 + 4 * ROWS // BLOCK,))],
        compiler_params=pltpu.CompilerParams(vmem_limit_bytes=24 * 2**20),
        name="update_and_error",
    )(merged, following, side, right_tiles)


def local(grad, error, momentum, warm_start):
    merged, following, side, right_tiles = iterate(*(pltpu.with_memory_space_constraint(v, pltpu.HBM) for v in (grad, error, momentum, jnp.swapaxes(warm_start, 1, 2))))
    error_next, momentum_next, update, basis_next = finish(merged, following, side, right_tiles)
    return error_next, momentum_next, update, jnp.swapaxes(basis_next, 1, 2)


def solution(mesh):
    split = P("rep", None, "fsdp", None)
    return jax.shard_map(
        local, mesh=mesh, in_specs=(split, split, split, P()),
        out_specs=(split, split, P(None, "fsdp", None), P()), check_vma=False)
```

```python
import functools

import jax
import jax.numpy as jnp
from jax import lax
from jax.experimental import pallas as pl
from jax.experimental.pallas import tpu as pltpu
from jax.sharding import PartitionSpec as P

MESH = pl.DeviceIdType.MESH
f32 = jnp.float32
bf16 = jnp.bfloat16

RANK = 64
ROWS = 512
COLS = 1024
CHUNK = 128
CHUNKS = ROWS // CHUNK
CHIPS = 64
OFFSETS = sorted(
    ((dz, dx, dy) for dz in range(4) for dx in range(4) for dy in range(4) if dz or dx or dy),
    key=lambda o: -sum(min(d, 4 - d) for d in o))
PLANE = [o for o in OFFSETS if o[0] == 0]
NN = (((1,), (0,)), ((), ()))
NT = (((1,), (1,)), ((), ()))
TN = (((0,), (0,)), ((), ()))


def split3(x):
    high = x.astype(bf16)
    rest = x - high.astype(f32)
    mid = rest.astype(bf16)
    low = (rest - mid.astype(f32)).astype(bf16)
    return high, mid, low


def whole(tiles):
    return jnp.concatenate(
        [jnp.concatenate([tiles[a * 8 + b] for b in range(8)], axis=1) for a in range(8)], axis=0)


def dot6(a, w, dims):
    n = a[0].shape[0]
    dot = functools.partial(lax.dot_general, dimension_numbers=dims, preferred_element_type=f32)
    s1 = dot(jnp.concatenate(a, axis=0), w[0])
    s2 = dot(jnp.concatenate(a[:2], axis=0), w[1])
    s3 = dot(a[0], w[2])
    return ((s1[2 * n:] + s2[n:]) + s3) + (s1[n:2 * n] + s2[:n]) + s1[:n]


def inverse_lower_factor(gram):
    n = RANK
    row_id = lax.broadcasted_iota(jnp.int32, (n, n), 0)
    col_id = lax.broadcasted_iota(jnp.int32, (n, n), 1)
    diagonal = row_id == col_id
    trace = jnp.sum(jnp.where(diagonal, gram, 0.0))
    a = jnp.concatenate(
        [gram + jnp.where(diagonal, 0.0001 * trace / n, 0.0), jnp.where(diagonal, 1.0, 0.0).astype(f32)], axis=1)
    done = []
    for k in range(0, n, 8):
        cols = [jnp.broadcast_to(a[:, k + j:k + j + 1], a.shape) for j in range(8)]
        rows = [a[j:j + 1, :] for j in range(8)]
        for j in range(8):
            inv = lax.rsqrt(cols[j][j:j + 1, :])
            rows[j] = rows[j] * inv
            cols[j] = cols[j] * inv
            for l in range(j + 1, 8):
                factor = cols[j][l:l + 1, :]
                rows[l] = rows[l] - factor * rows[j]
                cols[l] = cols[l] - factor * cols[j]
        done += rows
        a = a[8:]
        if k + 8 < n:
            for j in range(8):
                a = a - cols[j][8:] * rows[j]
    return jnp.concatenate(done, axis=0)[:, n:]


def iterate_kernel(grad, error, momentum, warm, merged_out, following_out, side_out, right_out,
                   g_buf, e_buf, m_buf, w_buf, landed, parts, across, warm_parts,
                   f_slots, y_tiles, y_terms, y_full, g_tiles, g_terms, g_full, theirs_side, theirs_right,
                   load_sem, warm_sem, second, third, fourth, swap_send, swap_recv, f_send, f_recv, rs_send, rs_recv, ag_send, ag_recv,
                   gram_send, gram_recv, gram_z_send, gram_z_recv, end_send, end_recv):
    rep = lax.axis_index("rep")
    fsdp = lax.axis_index("fsdp")
    z, core = rep // 2, lax.rem(rep, 2)
    x, y = fsdp // 4, lax.rem(fsdp, 4)
    chip = z * 16 + fsdp
    partner = (rep + 1 - 2 * core, fsdp)

    def load(role, q):
        p = core if role else 1 - core
        rows = pl.ds(q * CHUNK, CHUNK)
        return [
            pltpu.make_async_copy(ref.at[0, p, rows], buf.at[role, rows], load_sem.at[i, role, q])
            for i, (ref, buf) in enumerate(((grad, g_buf), (error, e_buf), (momentum, m_buf)))
        ]

    zs = [lax.rem(z + d, 4) for d in range(4)]
    xs = [lax.rem(x + d, 4) for d in range(4)]
    ys = [lax.rem(y + d, 4) for d in range(4)]
    lines = [(zs[d] * 2 + core, fsdp) for d in (1, 2, 3)]
    lines += [(rep, xs[d] * 4 + y) for d in (1, 2, 3)]
    lines += [(rep, x * 4 + ys[d]) for d in (1, 2, 3)]

    beside = [lines[i] for i in (0, 2, 3, 5, 6, 8)]

    def tell(sem, devices):
        for device in devices:
            pl.semaphore_signal(sem, inc=1, device_id=device, device_id_type=MESH)

    barrier = pltpu.get_barrier_semaphore()
    tell(barrier, beside)
    pl.semaphore_signal(barrier, inc=1, device_id=partner, device_id_type=MESH)

    warm_copy = pltpu.make_async_copy(warm.at[core], w_buf, warm_sem)
    def read(*chunks):
        for role, q in chunks:
            for copy in load(role, q):
                copy.start()

    read((0, 0), (0, 1), (0, 2))
    warm_copy.start()

    def chip_at(offset):
        dz, dx, dy = offset
        return zs[dz], xs[dx] * 4 + ys[dy]

    def swap(q):
        rows = pl.ds(q * CHUNK, CHUNK)
        return pltpu.make_async_remote_copy(
            src_ref=merged_out.at[1 - core, rows], dst_ref=landed.at[rows],
            send_sem=swap_send.at[q], recv_sem=swap_recv.at[q],
            device_id=partner, device_id_type=MESH)

    def merge(role, q):
        for copy in load(role, q):
            copy.wait()
        p = core if role else 1 - core
        rows = slice(q * CHUNK, (q + 1) * CHUNK)
        following = 0.9 * m_buf[role, rows] + g_buf[role, rows].astype(f32)
        following_out[p, rows] = following
        value = following + e_buf[role, rows]
        merged_out[p, rows] = value
        return value

    def f_copy(it, q, dz):
        block = f_slots.at[it, q, z]
        return pltpu.make_async_remote_copy(
            src_ref=block, dst_ref=block, send_sem=f_send.at[it, q, dz - 1], recv_sem=f_recv.at[it, q],
            device_id=(zs[dz] * 2 + core, fsdp), device_id_type=MESH)

    def f_all(it, q):
        three = f_slots.at[it, q, pl.ds(0, 3)]
        return pltpu.make_async_copy(three, three, f_recv.at[it, q])

    def send_factor(it, q, value):
        f_slots[it, q, z] = value
        for dz in (2, 1, 3):
            f_copy(it, q, dz).start()

    for q in range(CHUNKS):
        merge(0, q)
        read(*(((0, 3),), ((1, 0),), ((1, 1),), ((1, 2), (1, 3)))[q])
        if q == 0:
            pl.semaphore_wait(barrier, 7)
        swap(q).start()
        if q == 0:
            tell(second, beside)
    warm_copy.wait()
    for i, part in enumerate(split3(w_buf[...])):
        warm_parts[i] = part

    for q in range(CHUNKS):
        rows = slice(q * CHUNK, (q + 1) * CHUNK)
        own = merge(1, q)
        swap(q).wait_recv()
        block = split3((own + landed[rows]) * 0.125)
        for i in range(3):
            parts[i, rows] = block[i]
        value = dot6([warm_parts[i] for i in range(3)], block, NT)
        if q == 0:
            pl.semaphore_wait(second, 6)
        send_factor(0, q, value)
        if q == 0:
            tell(third, lines)
    pl.semaphore_wait(third, 9)
    tell(fourth, lines)

    def gram_copy(it, offset):
        _, pf = chip_at(offset)
        return pltpu.make_async_remote_copy(
            src_ref=g_tiles.at[it, z], dst_ref=g_terms.at[it, fsdp],
            send_sem=gram_send.at[it], recv_sem=gram_recv.at[it],
            device_id=(rep, pf), device_id_type=MESH)

    def gram_z_copy(it, dz):
        return pltpu.make_async_remote_copy(
            src_ref=g_full.at[it, z], dst_ref=g_full.at[it, z],
            send_sem=gram_z_send.at[it], recv_sem=gram_z_recv.at[it],
            device_id=(zs[dz] * 2 + core, fsdp), device_id_type=MESH)

    def rs_copy(it, k):
        pz, pf = chip_at(OFFSETS[k])
        return pltpu.make_async_remote_copy(
            src_ref=y_tiles.at[it, pz * 16 + pf], dst_ref=y_terms.at[it, k],
            send_sem=rs_send.at[it], recv_sem=rs_recv.at[it], device_id=(pz * 2 + core, pf), device_id_type=MESH)

    def ag_copy(it, k):
        pz, pf = chip_at(OFFSETS[k])
        return pltpu.make_async_remote_copy(
            src_ref=y_full.at[it, chip], dst_ref=y_full.at[it, chip],
            send_sem=ag_send.at[it], recv_sem=ag_recv.at[it, OFFSETS[k][0]], device_id=(pz * 2 + core, pf), device_id_type=MESH)

    def all_of(ref, sem):
        return pltpu.make_async_copy(ref, ref, sem)

    def gathered(it, d):
        return all_of(y_full.at[it, pl.ds(0, 16 if d else 15)], ag_recv.at[it, d])

    def right_copy(d):
        part = pl.ds(zs[(4 - d) % 4] * 16, 16)
        return pltpu.make_async_remote_copy(
            src_ref=y_full.at[1, part], dst_ref=theirs_right.at[part],
            send_sem=end_send.at[d], recv_sem=end_recv.at[d], device_id=partner, device_id_type=MESH)

    side_copy = pltpu.make_async_remote_copy(
        src_ref=side_out.at[core], dst_ref=theirs_side,
        send_sem=end_send.at[4], recv_sem=end_recv.at[4], device_id=partner, device_id_type=MESH)

    for it in range(2):
        pieces = []
        term = None
        for q in range(CHUNKS):
            f_all(it, q).wait()
            piece = split3(jnp.sum(f_slots[it, q], axis=0))
            pieces.append(piece)
            more = dot6(piece, [parts[i, q * CHUNK:(q + 1) * CHUNK] for i in range(3)], NN)
            term = more if q == 0 else term + more
            if q < CHUNKS - 1:
                square = dot6(piece, piece, NT)
                gram = square if q == 0 else gram + square
        for a in range(8):
            for b in range(8):
                y_tiles[it, a * 8 + b] = term[a * 8:(a + 1) * 8, b * 128:(b + 1) * 128]
        y_terms[it, CHIPS - 1] = y_tiles[it, chip]
        if it == 0:
            pl.semaphore_wait(fourth, 9)
        for k in range(CHIPS - 1):
            rs_copy(it, k).start()

        factor_parts = tuple(jnp.concatenate([piece[i] for piece in pieces], axis=1) for i in range(3))
        gram = gram + dot6(piece, piece, NT)
        packed = jnp.concatenate([gram[:32], gram[32:]], axis=1)
        for i in range(4):
            g_tiles[it, i] = packed[i * 8:(i + 1) * 8]
        g_terms[it, fsdp] = g_tiles[it, z]
        for offset in PLANE:
            gram_copy(it, offset).start()
        if it == 0:
            for i in range(3):
                across[i] = parts[i].T

        all_of(g_terms.at[it, pl.ds(0, 15)], gram_recv.at[it]).wait()
        g_full[it, z] = jnp.sum(g_terms[it], axis=0)
        for dz in (2, 1, 3):
            gram_z_copy(it, dz).start()

        all_of(y_terms.at[it, pl.ds(0, CHIPS - 1)], rs_recv.at[it]).wait()
        y_full[it, chip] = sum(jnp.sum(y_terms[it, i * 16:(i + 1) * 16], axis=0) for i in range(4))
        for k in range(CHIPS - 1):
            ag_copy(it, k).start()

        all_of(g_full.at[it, pl.ds(0, 3)], gram_z_recv.at[it]).wait()
        packed = jnp.concatenate([g_full[it, i] for i in range(4)], axis=0)
        inverse = inverse_lower_factor(jnp.concatenate([packed[:, :RANK], packed[:, RANK:]], axis=0))
        inverse_parts = split3(inverse)
        if it == 1:
            side_out[core, :, :ROWS] = dot6(inverse_parts, factor_parts, NN)
            side_out[core, :, ROWS:] = jnp.concatenate([inverse, jnp.zeros_like(inverse)], axis=1)
            side_copy.start()

        for d in (0, 1, 3, 2):
            gathered(it, d).wait()
            if it == 1:
                right_copy(d).start()
        if it == 0:
            total = split3(whole(y_full[0]))
            for h in range(0, CHUNKS, 2):
                wide = dot6(total, [across[i, :, h * CHUNK:(h + 2) * CHUNK] for i in range(3)], NN)
                wide = dot6(inverse_parts, split3(wide), NN)
                send_factor(1, h, wide[:, :CHUNK])
                send_factor(1, h + 1, wide[:, CHUNK:])

    right_out[core] = y_full[1]
    side_copy.wait()
    side_out[1 - core] = theirs_side[...]
    for q in range(CHUNKS):
        swap(q).wait_send()
    for it in range(2):
        for q in range(CHUNKS):
            for dz in (1, 2, 3):
                f_copy(it, q, dz).wait_send()
        all_of(y_terms.at[it, pl.ds(0, CHIPS - 1)], rs_send.at[it]).wait()
        all_of(y_full.at[it, pl.ds(0, CHIPS - 1)], ag_send.at[it]).wait()
        all_of(g_terms.at[it, pl.ds(0, 15)], gram_send.at[it]).wait()
        all_of(g_full.at[it, pl.ds(0, 3)], gram_z_send.at[it]).wait()
    for d in (0, 1, 3, 2):
        right_copy(d).wait()
    right_out[1 - core] = theirs_right[...]


def iterate(grad, error, momentum, warm):
    vmem = pl.BlockSpec(memory_space=pltpu.VMEM)
    hbm = pl.BlockSpec(memory_space=pltpu.HBM)
    dma = pltpu.SemaphoreType.DMA
    return pl.pallas_call(
        iterate_kernel,
        out_shape=(
            jax.ShapeDtypeStruct((2, ROWS, COLS), f32), jax.ShapeDtypeStruct((2, ROWS, COLS), f32),
            jax.ShapeDtypeStruct((2, RANK, ROWS + 128), f32), jax.ShapeDtypeStruct((2, CHIPS, 8, 128), f32)),
        in_specs=[hbm, hbm, hbm, hbm],
        out_specs=(vmem, vmem, vmem, vmem),
        scratch_shapes=[
            pltpu.VMEM((2, ROWS, COLS), bf16),
            pltpu.VMEM((2, ROWS, COLS), f32),
            pltpu.VMEM((2, ROWS, COLS), f32),
            pltpu.VMEM((RANK, COLS), f32),
            pltpu.VMEM((ROWS, COLS), f32),
            pltpu.VMEM((3, ROWS, COLS), bf16),
            pltpu.VMEM((3, COLS, ROWS), bf16),
            pltpu.VMEM((3, RANK, COLS), bf16),
            pltpu.VMEM((2, CHUNKS, 4, RANK, CHUNK), f32),
            pltpu.VMEM((2, CHIPS, 8, 128), f32),
            pltpu.VMEM((2, CHIPS, 8, 128), f32),
            pltpu.VMEM((2, CHIPS, 8, 128), f32),
            pltpu.VMEM((2, 4, 8, 128), f32),
            pltpu.VMEM((2, 16, 8, 128), f32),
            pltpu.VMEM((2, 4, 8, 128), f32),
            pltpu.VMEM((RANK, ROWS + 128), f32),
            pltpu.VMEM((CHIPS, 8, 128), f32),
            dma((3, 2, CHUNKS)), dma,
            pltpu.SemaphoreType.REGULAR, pltpu.SemaphoreType.REGULAR, pltpu.SemaphoreType.REGULAR,
            dma((CHUNKS,)), dma((CHUNKS,)),
            dma((2, CHUNKS, 3)), dma((2, CHUNKS)),
            dma((2,)), dma((2,)),
            dma((2,)), dma((2, 4)),
            dma((2,)), dma((2,)),
            dma((2,)), dma((2,)),
            dma((5,)), dma((5,)),
        ],
        compiler_params=pltpu.CompilerParams(
            collective_id=0, has_side_effects=True, vmem_limit_bytes=40 * 2**20),
        name="power_iterations",
    )(grad, error, momentum, warm)


BLOCK = 256


def finish_kernel(merged, following, side, right_tiles, error_next, momentum_next, update, basis_next,
                  basis, delta_buf, error_buf, sems):
    steps = [(p, i) for p in range(2) for i in range(ROWS // BLOCK)]
    copies = [
        pltpu.make_async_copy(following, momentum_next.at[0], sems.at[0]),
        pltpu.make_async_copy(basis, basis_next, sems.at[1]),
    ]
    copies[0].start()
    for n, (p, i) in enumerate(steps):
        rows = slice(i * BLOCK, (i + 1) * BLOCK)
        part = pl.ds(i * BLOCK, BLOCK)
        if i == 0:
            inverse = split3(side[p, :, ROWS:ROWS + RANK])
            value = dot6(inverse, split3(whole(right_tiles[p])), NN)
            basis[p] = value
            b = split3(value)
            right = jnp.concatenate([b[0], b[1], b[0], b[2], b[0], b[1]], axis=0)
        u = split3(side[p, :, rows])
        left = jnp.concatenate([u[0], u[0], u[1], u[0], u[2], u[1]], axis=0)
        delta = lax.dot_general(left, right, TN, preferred_element_type=f32)
        delta_buf[p, rows] = delta
        error_buf[p, rows] = merged[p, rows] - delta
        new = [
            pltpu.make_async_copy(delta_buf.at[p, part], update.at[p, part], sems.at[2 + 2 * n]),
            pltpu.make_async_copy(error_buf.at[p, part], error_next.at[0, p, part], sems.at[3 + 2 * n]),
        ]
        for copy in new:
            copy.start()
        copies += new
    copies[1].start()
    for copy in copies:
        copy.wait()


def finish(merged, following, side, right_tiles):
    vmem = pl.BlockSpec(memory_space=pltpu.VMEM)
    hbm = pl.BlockSpec(memory_space=pltpu.HBM)
    kept = jax.ShapeDtypeStruct((1, 2, ROWS, COLS), f32)
    return pl.pallas_call(
        finish_kernel,
        out_shape=(kept, kept, jax.ShapeDtypeStruct((2, ROWS, COLS), f32), jax.ShapeDtypeStruct((2, RANK, COLS), f32)),
        in_specs=[vmem, vmem, vmem, vmem],
        out_specs=(hbm, hbm, hbm, hbm),
        scratch_shapes=[
            pltpu.VMEM((2, RANK, COLS), f32),
            pltpu.VMEM((2, ROWS, COLS), f32), pltpu.VMEM((2, ROWS, COLS), f32),
            pltpu.SemaphoreType.DMA((2 + 4 * ROWS // BLOCK,))],
        compiler_params=pltpu.CompilerParams(vmem_limit_bytes=24 * 2**20),
        name="update_and_error",
    )(merged, following, side, right_tiles)


def local(grad, error, momentum, warm_start):
    merged, following, side, right_tiles = iterate(*(pltpu.with_memory_space_constraint(v, pltpu.HBM) for v in (grad, error, momentum, jnp.swapaxes(warm_start, 1, 2))))
    error_next, momentum_next, update, basis_next = finish(merged, following, side, right_tiles)
    return error_next, momentum_next, update, jnp.swapaxes(basis_next, 1, 2)


def solution(mesh):
    split = P("rep", None, "fsdp", None)
    return jax.shard_map(
        local, mesh=mesh, in_specs=(split, split, split, P()),
        out_specs=(split, split, P(None, "fsdp", None), P()), check_vma=False)
```
